512 devices in a mesh: blk: 16 (over z, y_hi), pair: 32 (over y_lo, x, core).
Axes of the slice: x: 4, y: 8 (y_hi: 2, y_lo: 4; y = y_hi * 4 + y_lo), z: 8, core: 2. Of those that a mesh axis runs over, the one named last changes fastest.
Arguments:
- integrals: float32 [16, 32, 25, 25600], P('blk', 'pair'), may hold values from -0.0390625 to 0.0390625
- amplitudes: float32 [25600, 256], P('blk'), may hold values from -6 to 6
- block_map: int32 [16, 32, 2], P('blk', 'pair'), may hold values from 0 to 31, as said below
- eps_vir: float32 [160], replicated, may hold values from 0.2 to 2
- eps_occ: float32 [16], replicated, may hold values from -1.5 to -0.1
Outputs:
- update: float32 [16, 32, 25, 256], P('blk', 'pair')
The draws below stay inside these ranges and needn't reach their ends.
Inputs may be any that keep to these rules, and one draw needn't show every extreme that they name: `block_map`: each device's two blocks differ; the device whose pair index differs by 32/2 (same blk index) holds the same two blocks in swapped order; no two devices hold the same ordered pair of blocks. `eps_vir`: the virtual energies are positive and the occupied ones negative, so every denominator is 0.6 or more.
All inputs are finite; a program needn't handle non-finite values.
Results may differ from the reference program's by a relative error of at most 0.00011.
Values sent between devices are 32-bit elements; how exact they have to be, the bound alone decides.
A program may use at most 128 MiB of HBM per device.

```python
import math
import jax
import jax.numpy as jnp
import numpy as np
from jax import lax

VIRTUALS = 160
OCCUPIED = 16
BLOCK_SIDE = 5
BLOCK_COUNT = 32
SB_ROWS = 25
VIRT_PAIRS = 25600
OCC_PAIRS = 256
N_BLK = 16
N_PAIR = 32


def draw_block_map(key, part):
    key = jax.random.fold_in(key, 11)
    first_key, second_key = jax.random.split(key)
    upper, lower = np.triu_indices(BLOCK_COUNT, 1)
    upper_table = jnp.asarray(upper, dtype=jnp.int32)
    lower_table = jnp.asarray(lower, dtype=jnp.int32)
    half = N_BLK * N_PAIR // 2
    order = jax.random.permutation(first_key, upper_table.shape[0]).astype(jnp.int32)
    wanted = BLOCK_COUNT - 2
    where_wanted = jnp.argmax(order == wanted)
    order = order.at[where_wanted].set(order[0]).at[0].set(wanted)
    chosen = order[:half]
    first_block = upper_table[chosen]
    second_block = lower_table[chosen]
    flipped = jax.random.randint(second_key, (half,), 0, 2, dtype=jnp.int32)
    big_side = jnp.where(flipped == 1, second_block, first_block)
    small_side = jnp.where(flipped == 1, first_block, second_block)
    front = jnp.stack([big_side, small_side], -1).reshape(N_BLK, N_PAIR // 2, 2)
    back = jnp.stack([small_side, big_side], -1).reshape(N_BLK, N_PAIR // 2, 2)
    return jnp.concatenate([front, back], 1).astype(jnp.int32)


def block_scale(rng, shape, cuts, least, high):
    factor_of = 1.0
    for dim, blocks in cuts:
        draws = jax.random.uniform(jax.random.fold_in(jax.random.fold_in(rng, 6), dim), (blocks,), jnp.float32, least / len(cuts), high / len(cuts))
        factor_of = factor_of * jnp.repeat(jnp.exp(draws), shape[dim] // blocks).reshape((-1,) + (1,) * (len(shape) - 1 - dim))
    return factor_of


def noise(rng, shape, width, most, cuts=(), held_as=jnp.bfloat16):
    gain = block_scale(rng, shape, cuts, -0.22, 0.18) if cuts else 1.0
    result = jax.random.normal(rng, shape, jnp.float32) * width * gain
    return jnp.minimum(jnp.maximum(result, -most), most).astype(held_as)


def setup_inputs(seed: int = 0) -> dict:
    splits = jax.random.split(jax.random.key(seed), 6)
    integrals = noise(splits[0], (N_BLK, N_PAIR, SB_ROWS, VIRT_PAIRS), VIRT_PAIRS ** -0.5, 0.0390625, ((0, 16), (1, 32)), jnp.float32)
    amplitudes = noise(splits[1], (VIRT_PAIRS, OCC_PAIRS), 1.0, 6.0, ((0, 16),), jnp.float32)
    block_map = draw_block_map(jax.random.fold_in(splits[5], 71), 0)
    eps_vir = jnp.clip(jnp.exp(jax.random.uniform(splits[3], (VIRTUALS,), jnp.float32, math.log(0.2), math.log(2.0))), 0.2, 2.0)
    eps_occ = jnp.clip(jax.random.uniform(splits[4], (OCCUPIED,), jnp.float32, -1.5, -0.1), -1.5, -0.1)
    return {"integrals": integrals, "amplitudes": amplitudes, "block_map": block_map, "eps_vir": eps_vir, "eps_occ": eps_occ}


def reference(integrals, amplitudes, block_map, eps_vir, eps_occ):
    flat = integrals.reshape(N_BLK * N_PAIR * SB_ROWS, VIRT_PAIRS)
    ladder = jnp.dot(flat, amplitudes, precision=lax.Precision.HIGHEST, preferred_element_type=jnp.float32)
    ladder = ladder.reshape(N_BLK, N_PAIR, BLOCK_SIDE, BLOCK_SIDE, OCCUPIED, OCCUPIED)
    mirrored = jnp.roll(ladder, N_PAIR // 2, axis=1).transpose(0, 1, 3, 2, 5, 4)
    offsets = jnp.arange(BLOCK_SIDE, dtype=jnp.int32)
    a_index = (block_map[:, :, 0:1] * BLOCK_SIDE + offsets).astype(jnp.int32)
    b_index = (block_map[:, :, 1:2] * BLOCK_SIDE + offsets).astype(jnp.int32)
    energy_a = eps_vir[a_index]
    energy_b = eps_vir[b_index]
    denominator = ((energy_a[:, :, :, None, None, None] + energy_b[:, :, None, :, None, None]) - eps_occ[:, None]) - eps_occ
    update = (ladder + mirrored) / denominator
    return update.reshape(N_BLK, N_PAIR, SB_ROWS, OCC_PAIRS)
```

```python
import functools

import jax
import jax.numpy as jnp
from jax import lax
from jax.experimental import pallas as pl
from jax.experimental.pallas import tpu as pltpu
from jax.sharding import PartitionSpec as P

MESH = pl.DeviceIdType.MESH

OCCUPIED = 16
SIDE = 5
ROWS = 25
FULL = 24
SLOT = 32
COLS = 256
WINDOW = 3200
MAIN = 192
EXTRA = 8
HALF = 96
FIRST = EXTRA + HALF
PIECE = FIRST + HALF
X, Y, Z = 4, 8, 8
SENDS = ((2, 1, 0), (6, -1, 0), (3, 0, 1), (5, 0, -1), (1, -1, 1), (7, 1, -1), (4, 2, 0))
CHUNKS = ((0, FIRST), (FIRST, HALF))


def device(z, y, x, core):
    return (z * 2 + y // 4, (y % 4) * 8 + x * 2 + core)


def kernel(
    v_ref, t_ref, map_ref, vir_ref, occ_ref, out_ref,
    vbuf, last, packed, vlast, tbuf, acc, give, parts, mine, other, den, turn,
    tin_send, tin_recv, ring_send, ring_recv, core_send, core_recv,
    v_send, v_recv, v_own, last_send, last_recv, last_own, part_send, part_recv, mir_send, mir_recv,
):
    blk, pair = lax.axis_index("blk"), lax.axis_index("pair")
    z, y_hi = blk // 2, blk % 2
    y_lo, x, core = pair // 8, (pair // 2) % 4, pair % 2
    y = y_hi * 4 + y_lo
    colour = (3 * z + 2 * x + 1) % 8

    def at(dx=0, dy=0, dz=0):
        return device((z + dz + Z) % Z, (y + dy + Y) % Y, (x + dx + X) % X, core)

    sibling = device(z, y, x, 1 - core)
    up, down = at(dy=1), at(dy=-1)
    twin = device(z, y_hi * 4 + (y_lo + 2) % 4, x, core)
    source = device(colour, y, x, core)
    target = device((3 * (z - 2 * x - 1) + 72) % 8, y, x, core)

    last_row = pltpu.make_async_copy(v_ref.at[0, 0, pl.ds(FULL, 1), :], last, last_own.at[0])
    last_row.start()

    barrier = pltpu.get_barrier_semaphore()
    greet = [sibling, up, down, twin, source] + [at(dx=-dx, dz=-dz) for _, dx, dz in SENDS]
    for peer in greet:
        pl.semaphore_signal(barrier, inc=1, device_id=peer, device_id_type=MESH)
    pl.semaphore_wait(barrier, len(greet))

    def remote(src, dst, send, recv, peer):
        return pltpu.make_async_remote_copy(
            src_ref=src, dst_ref=dst, send_sem=send, recv_sem=recv, device_id=peer, device_id_type=MESH
        )

    main_at = pl.multiple_of(y_hi * 64 + y_lo * 384 + core * MAIN, 8)
    extra_at = pl.multiple_of((1 - y_hi) * 1536 + 8 * (2 * y_lo + core), 8)
    home = tbuf.at[y, core]
    tin = [
        remote(t_ref.at[pl.ds(extra_at, EXTRA)], home.at[pl.ds(0, EXTRA)], tin_send.at[0], tin_recv.at[0], target),
        remote(t_ref.at[pl.ds(main_at, HALF)], home.at[pl.ds(EXTRA, HALF)], tin_send.at[1], tin_recv.at[1], target),
        remote(
            t_ref.at[pl.ds(pl.multiple_of(main_at + HALF, 8), HALF)], home.at[pl.ds(FIRST, HALF)],
            tin_send.at[2], tin_recv.at[2], target,
        ),
    ]
    for copy in tin:
        copy.start()

    def columns(step):
        return pl.ds(pl.multiple_of(((colour + step) % 8) * WINDOW, 128), WINDOW)

    vout = []
    for i, (step, dx, dz) in enumerate(SENDS):
        vout.append(
            remote(
                v_ref.at[0, 0, pl.ds(0, FULL), columns(step)], vbuf.at[i + 1],
                v_send.at[i], v_recv.at[i], at(dx=dx, dz=dz),
            )
        )
    for copy in vout:
        copy.start()
    own = pltpu.make_async_copy(v_ref.at[0, 0, pl.ds(0, FULL), columns(0)], vbuf.at[0], v_own.at[0])
    own.start()

    last_row.wait()
    for k in range(8):
        for j in range(25):
            packed[k, j : j + 1, :] = last[0:1, (25 * k + j) * 128 : (25 * k + j + 1) * 128]
    for i, (step, dx, dz) in enumerate(SENDS):
        copy = remote(
            packed.at[(colour + step) % 8], vlast.at[i + 1], last_send.at[i], last_recv.at[i], at(dx=dx, dz=dz)
        )
        copy.start()
        vout.append(copy)
    vlast[0] = packed[colour]

    lane = lax.broadcasted_iota(jnp.int32, (1, COLS), 1)
    occ_i = jnp.zeros((1, COLS), jnp.float32)
    occ_j = jnp.zeros((1, COLS), jnp.float32)
    for i in range(OCCUPIED):
        occ_i = jnp.where(lane // OCCUPIED == i, occ_ref[i], occ_i)
        occ_j = jnp.where(lane % OCCUPIED == i, occ_ref[i], occ_j)
    for s in range(SIDE):
        for t in range(SIDE):
            both = vir_ref[map_ref[0, 0, 0] * SIDE + s] + vir_ref[map_ref[0, 0, 1] * SIDE + t]
            r = s * SIDE + t
            den[r : r + 1, :] = (both - occ_i) - occ_j
    row = lax.broadcasted_iota(jnp.int32, (COLS, COLS), 0)
    col = lax.broadcasted_iota(jnp.int32, (COLS, COLS), 1)
    turn[...] = ((row // OCCUPIED == col % OCCUPIED) & (row % OCCUPIED == col // OCCUPIED)).astype(jnp.bfloat16)

    started = []

    def ring(way, hop, chunk):
        at_y = (y - hop + Y) % Y if way == 0 else (y + hop) % Y
        start, size = CHUNKS[chunk]
        ref = tbuf.at[at_y, core, pl.ds(start, size)]
        return remote(ref, ref, ring_send.at[way, hop, chunk], ring_recv.at[way, hop, chunk], up if way == 0 else down)

    def arrived(way, hop, chunk):
        at_y = (y - hop - 1 + Y) % Y if way == 0 else (y + hop + 1) % Y
        start, size = CHUNKS[chunk]
        ref = tbuf.at[at_y, core, pl.ds(start, size)]
        return remote(ref, ref, ring_send.at[way, hop, chunk], ring_recv.at[way, hop, chunk], up if way == 0 else down)

    def place_y(place):
        step = (0, -1, -2, -3, 1, 2, 3, 4)[place]
        return (y + step + Y) % Y

    def across(place, chunk):
        start, size = CHUNKS[chunk]
        ref = tbuf.at[place_y(place), core, pl.ds(start, size)]
        return remote(ref, ref, core_send.at[place, chunk], core_recv.at[place, chunk], sibling)

    def across_in(place, chunk):
        start, size = CHUNKS[chunk]
        ref = tbuf.at[place_y(place), 1 - core, pl.ds(start, size)]
        return remote(ref, ref, core_send.at[place, chunk], core_recv.at[place, chunk], sibling)

    def go(copy):
        copy.start()
        started.append(copy)

    for chunk in range(2):
        for copy in (tin[:2], tin[2:])[chunk]:
            copy.wait_recv()
        go(ring(0, 0, chunk))
        go(ring(1, 0, chunk))
        go(across(0, chunk))
    for hop in range(1, 4):
        for chunk in range(2):
            for way in range(2):
                arrived(way, hop - 1, chunk).wait_recv()
                if hop < 3 or way == chunk:
                    go(ring(way, hop, chunk))
                go(across(hop + 3 * way, chunk))
    for way in range(2):
        arrived(way, 3, way).wait_recv()
        go(across(7, way))

    own.wait()
    for copy in vout:
        copy.wait_recv()

    def split(value):
        high = value.astype(jnp.bfloat16)
        return high, (value - high.astype(jnp.float32)).astype(jnp.bfloat16)

    def product(v, t):
        v_high, v_low = split(v)
        t_high, t_low = split(t)
        dot = functools.partial(jnp.dot, preferred_element_type=jnp.float32)
        return dot(v_high, t_high) + (dot(v_low, t_high) + dot(v_high, t_low))

    def gathered(tile, tiles):
        first = pl.multiple_of(128 * tile, 128)
        v = vbuf[:, :, pl.ds(first, 128 * tiles)].reshape(8 * FULL, 128 * tiles)
        ends = [vlast[:, pl.ds(tile + k, 1), :].reshape(8, 128) for k in range(tiles)]
        return jnp.concatenate([v, jnp.concatenate(ends, axis=1)], axis=0)

    for place in (0, 1, 4, 2, 5, 3, 6, 7):
        for chunk in range(2):
            across_in(place, chunk).wait_recv()
        at_y = place_y(place)
        first = pl.multiple_of(384 * at_y + 128 * (at_y // 4), 128)
        t = tbuf[at_y, :, EXTRA:PIECE, :].reshape(2 * MAIN, COLS)
        tile = 3 * at_y + at_y // 4
        v = gathered(tile, 3)
        if place == 0:
            acc[...] = product(v, t)
        else:
            acc[...] += product(v, t)
    t = tbuf[:, :, 0:EXTRA, :].reshape(128, COLS)
    acc[...] += product(gathered(12, 1), t)

    back = []
    for i, (_, dx, dz) in enumerate(SENDS):
        give[i, 0:FULL, :] = acc[FULL * (i + 1) : FULL * (i + 2), :]
        give[i, FULL:ROWS, :] = acc[8 * FULL + i + 1 : 8 * FULL + i + 2, :]
        copy = remote(give.at[i], parts.at[i], part_send.at[i], part_recv.at[i], at(dx=-dx, dz=-dz))
        copy.start()
        back.append(copy)
    total = jnp.concatenate([acc[0:FULL, :], acc[8 * FULL : 8 * FULL + 8, :]], axis=0)
    for i in range(7):
        back[i].wait_recv()
        total = total + parts[i]
    mine[...] = total
    swap = remote(mine, other, mir_send.at[0], mir_recv.at[0], twin)
    swap.start()
    swap.wait_recv()
    dot = functools.partial(jnp.dot, preferred_element_type=jnp.float32)
    high, rest = split(other[...])
    mid = (other[...] - high.astype(jnp.float32)) - rest.astype(jnp.float32)
    turned = (dot(high, turn[...]) + dot(rest, turn[...])) + dot(mid.astype(jnp.bfloat16), turn[...])
    for s in range(SIDE):
        for t in range(SIDE):
            r, q = s * SIDE + t, t * SIDE + s
            out_ref[0, 0, r : r + 1, :] = (total[r : r + 1] + turned[q : q + 1]) / den[r : r + 1, :]

    for copy in tin + vout + started + back + [swap]:
        copy.wait_send()


def body(integrals, amplitudes, block_map, eps_vir, eps_occ):
    smem = pl.BlockSpec(memory_space=pltpu.SMEM)
    hbm = pl.BlockSpec(memory_space=pl.ANY)
    dma = pltpu.SemaphoreType.DMA
    f32 = jnp.float32
    return pl.pallas_call(
        kernel,
        out_shape=jax.ShapeDtypeStruct((1, 1, ROWS, COLS), f32),
        in_specs=[hbm, hbm, smem, smem, smem],
        out_specs=pl.BlockSpec(memory_space=pltpu.VMEM),
        scratch_shapes=[
            pltpu.VMEM((8, FULL, WINDOW), f32),
            pltpu.VMEM((1, 8 * WINDOW), f32),
            pltpu.VMEM((8, SLOT, 128), f32),
            pltpu.VMEM((8, SLOT, 128), f32),
            pltpu.VMEM((8, 2, PIECE, COLS), f32),
            pltpu.VMEM((8 * ROWS, COLS), f32),
            pltpu.VMEM((7, SLOT, COLS), f32),
            pltpu.VMEM((7, SLOT, COLS), f32),
            pltpu.VMEM((SLOT, COLS), f32),
            pltpu.VMEM((SLOT, COLS), f32),
            pltpu.VMEM((SLOT, COLS), f32),
            pltpu.VMEM((COLS, COLS), jnp.bfloat16),
            dma((3,)), dma((3,)),
            dma((2, 4, 2)), dma((2, 4, 2)),
            dma((8, 2)), dma((8, 2)),
            dma((7,)), dma((7,)), dma((1,)),
            dma((7,)), dma((7,)), dma((1,)),
            dma((7,)), dma((7,)),
            dma((1,)), dma((1,)),
        ],
        compiler_params=pltpu.CompilerParams(
            collective_id=0, has_side_effects=True, vmem_limit_bytes=40 * 2**20
        ),
        name="ladder",
    )(integrals, amplitudes, block_map, eps_vir, eps_occ)


def solution(mesh):
    in_specs = (P("blk", "pair", None, None), P("blk", None), P("blk", "pair", None), P(), P())
    out_specs = P("blk", "pair", None, None)
    return jax.shard_map(body, mesh=mesh, in_specs=in_specs, out_specs=out_specs, check_vma=False)
```

```python
import functools

import jax
import jax.numpy as jnp
from jax import lax
from jax.experimental import pallas as pl
from jax.experimental.pallas import tpu as pltpu
from jax.sharding import PartitionSpec as P

MESH = pl.DeviceIdType.MESH

OCCUPIED = 16
SIDE = 5
ROWS = 25
SLOT = 32
LANES = 128
TILES = 25
COLS = 256
MAIN = 192
EXTRA = 8
PIECE = EXTRA + MAIN
X, Y, Z = 4, 8, 8
SENDS = ((2, 1, 0), (6, -1, 0), (3, 0, 1), (5, 0, -1), (1, -1, 1), (7, 1, -1), (4, 2, 0))
CHUNKS = ((0, 56), (56, 48), (104, 48), (152, 48))
LAST_WAY = (0, 0, 1, 1)


def device(z, y, x, core):
    return (z * 2 + y // 4, (y % 4) * 8 + x * 2 + core)


def kernel(
    v_ref, t_ref, map_ref, vir_ref, occ_ref, out_ref,
    vbuf, tbuf, acc, give, parts, mine, other, den, turn,
    tin_send, tin_recv, ring_send, ring_recv, core_send, core_recv,
    v_send, v_recv, v_own, part_send, part_recv, mir_send, mir_recv,
):
    blk, pair = lax.axis_index("blk"), lax.axis_index("pair")
    z, y_hi = blk // 2, blk % 2
    y_lo, x, core = pair // 8, (pair // 2) % 4, pair % 2
    y = y_hi * 4 + y_lo
    colour = (3 * z + 2 * x + 1) % 8

    def at(dx=0, dy=0, dz=0):
        return device((z + dz + Z) % Z, (y + dy + Y) % Y, (x + dx + X) % X, core)

    sibling = device(z, y, x, 1 - core)
    up, down = at(dy=1), at(dy=-1)
    mirror = 2 - 4 * (y_lo // 2)
    twin = at(dy=mirror)
    source = device(colour, y, x, core)
    target = device((3 * (z - 2 * x - 1) + 72) % 8, y, x, core)

    barrier = pltpu.get_barrier_semaphore()
    greet = [sibling, up, down, twin, source] + [at(dx=-dx, dz=-dz) for _, dx, dz in SENDS]
    for peer in greet:
        pl.semaphore_signal(barrier, inc=1, device_id=peer, device_id_type=MESH)
    pl.semaphore_wait(barrier, len(greet))

    def remote(src, dst, send, recv, peer):
        return pltpu.make_async_remote_copy(
            src_ref=src, dst_ref=dst, send_sem=send, recv_sem=recv, device_id=peer, device_id_type=MESH
        )

    main_at = pl.multiple_of(y_hi * 64 + y_lo * 384 + core * MAIN, 8)
    extra_at = pl.multiple_of((1 - y_hi) * 1536 + 8 * (2 * y_lo + core), 8)
    home = tbuf.at[y, core]
    tin = [
        remote(t_ref.at[pl.ds(extra_at, EXTRA)], home.at[pl.ds(0, EXTRA)], tin_send.at[4], tin_recv.at[4], target)
    ]
    for chunk, (start, size) in enumerate(CHUNKS):
        skip = EXTRA if chunk == 0 else 0
        rows = pl.ds(pl.multiple_of(main_at + (start + skip - EXTRA), 8), size - skip)
        tin.append(
            remote(t_ref.at[rows], home.at[pl.ds(start + skip, size - skip)], tin_send.at[chunk], tin_recv.at[chunk], target)
        )
    for n, copy in enumerate(tin):
        copy.start()
    slots = vbuf.reshape(8, ROWS, TILES, 1, LANES)

    def columns(step):
        return v_ref.at[:, pl.ds(((colour + step) % 8) * TILES, TILES)]

    vout = []
    for i, (step, dx, dz) in enumerate(SENDS):
        vout.append(remote(columns(step), slots.at[i + 1], v_send.at[i], v_recv.at[i], at(dx=dx, dz=dz)))
    for copy in vout:
        copy.start()
    own = pltpu.make_async_copy(columns(0), slots.at[0], v_own.at[0])
    own.start()

    lane = lax.broadcasted_iota(jnp.int32, (1, COLS), 1)
    occ_i = jnp.zeros((1, COLS), jnp.float32)
    occ_j = jnp.zeros((1, COLS), jnp.float32)
    for i in range(OCCUPIED):
        occ_i = jnp.where((lane >> 4) == i, occ_ref[i], occ_i)
        occ_j = jnp.where((lane & 15) == i, occ_ref[i], occ_j)
    for s in range(SIDE):
        for t in range(SIDE):
            both = vir_ref[map_ref[0, 0, 0] * SIDE + s] + vir_ref[map_ref[0, 0, 1] * SIDE + t]
            r = s * SIDE + t
            den[r : r + 1, :] = (both - occ_i) - occ_j
    row = lax.broadcasted_iota(jnp.int32, (COLS, COLS), 0)
    col = lax.broadcasted_iota(jnp.int32, (COLS, COLS), 1)
    turn[...] = (((row >> 4) == (col & 15)) & ((row & 15) == (col >> 4))).astype(jnp.bfloat16)

    started = []

    def ring(way, hop, chunk):
        at_y = (y - hop + Y) % Y if way == 0 else (y + hop) % Y
        start, size = CHUNKS[chunk]
        ref = tbuf.at[at_y, core, pl.ds(start, size)]
        return remote(ref, ref, ring_send.at[way, hop, chunk], ring_recv.at[way, hop, chunk], up if way == 0 else down)

    def arrived(way, hop, chunk):
        at_y = (y - hop - 1 + Y) % Y if way == 0 else (y + hop + 1) % Y
        start, size = CHUNKS[chunk]
        ref = tbuf.at[at_y, core, pl.ds(start, size)]
        return remote(ref, ref, ring_send.at[way, hop, chunk], ring_recv.at[way, hop, chunk], up if way == 0 else down)

    def place_y(place):
        step = (0, -1, -2, -3, 1, 2, 3, 4)[place]
        return (y + step + Y) % Y

    def across(place, chunk):
        start, size = CHUNKS[chunk]
        ref = tbuf.at[place_y(place), core, pl.ds(start, size)]
        return remote(ref, ref, core_send.at[place, chunk], core_recv.at[place, chunk], sibling)

    def across_in(place, chunk):
        start, size = CHUNKS[chunk]
        ref = tbuf.at[place_y(place), 1 - core, pl.ds(start, size)]
        return remote(ref, ref, core_send.at[place, chunk], core_recv.at[place, chunk], sibling)

    def go(copy):
        copy.start()
        started.append(copy)

    tin[0].wait_recv()
    for chunk in range(len(CHUNKS)):
        tin[chunk + 1].wait_recv()
        go(ring(0, 0, chunk))
        go(ring(1, 0, chunk))
        go(across(0, chunk))
    for hop in range(1, 4):
        for chunk in range(len(CHUNKS)):
            for way in range(2):
                arrived(way, hop - 1, chunk).wait_recv()
                if hop < 3 or way == LAST_WAY[chunk]:
                    go(ring(way, hop, chunk))
                go(across(hop + 3 * way, chunk))
    own.wait()
    for copy in vout:
        copy.wait_recv()

    def split(value):
        high = value.astype(jnp.bfloat16)
        return high, (value - high.astype(jnp.float32)).astype(jnp.bfloat16)

    def product(v, t):
        v_high, v_low = split(v)
        t_high, t_low = split(t)
        dot = functools.partial(jnp.dot, preferred_element_type=jnp.float32)
        return dot(v_high, t_high) + (dot(v_low, t_high) + dot(v_high, t_low))

    def gathered(tile, tiles):
        return jnp.concatenate([vbuf[pl.ds(tile + k, 8 * ROWS, stride=TILES), :] for k in range(tiles)], axis=1)

    def add(place):
        for chunk in range(len(CHUNKS)):
            across_in(place, chunk).wait_recv()
        at_y = place_y(place)
        t = tbuf[at_y, :, EXTRA:PIECE, :].reshape(2 * MAIN, COLS)
        term = product(gathered(3 * at_y + at_y // 4, 3), t)
        if place == 0:
            acc[...] = term
        else:
            acc[...] += term

    for place in (0, 1, 4, 2, 5):
        add(place)
    for chunk in (0, 2, 1, 3):
        arrived(LAST_WAY[chunk], 3, chunk).wait_recv()
        go(across(7, chunk))
    for place in (3, 6, 7):
        add(place)
    t = tbuf[:, :, 0:EXTRA, :].reshape(128, COLS)
    acc[...] += product(gathered(12, 1), t)

    back = []
    for i, (_, dx, dz) in enumerate(SENDS):
        give[i, 0:ROWS, :] = acc[ROWS * (i + 1) : ROWS * (i + 2), :]
        copy = remote(give.at[i], parts.at[i], part_send.at[i], part_recv.at[i], at(dx=-dx, dz=-dz))
        copy.start()
        back.append(copy)
    total = acc[0:SLOT, :]
    for i in range(7):
        back[i].wait_recv()
        total = total + parts[i]
    mine[...] = total
    swap = remote(mine, other, mir_send.at[0], mir_recv.at[0], twin)
    swap.start()
    swap.wait_recv()
    dot = functools.partial(jnp.dot, preferred_element_type=jnp.float32)
    high, rest = split(other[...])
    mid = (other[...] - high.astype(jnp.float32)) - rest.astype(jnp.float32)
    turned = (dot(high, turn[...]) + dot(rest, turn[...])) + dot(mid.astype(jnp.bfloat16), turn[...])
    for s in range(SIDE):
        for t in range(SIDE):
            r, q = s * SIDE + t, t * SIDE + s
            out_ref[r] = (total[r : r + 1] + turned[q : q + 1]) / den[r : r + 1, :]

    for copy in tin + vout + started + back + [swap]:
        copy.wait_send()


def body(integrals, amplitudes, block_map, eps_vir, eps_occ):
    smem = pl.BlockSpec(memory_space=pltpu.SMEM)
    hbm = pl.BlockSpec(memory_space=pltpu.HBM)
    dma = pltpu.SemaphoreType.DMA
    f32 = jnp.float32
    tiles = jnp.transpose(integrals, (0, 2, 1, 3)).reshape(ROWS, 8 * TILES, 1, LANES)
    update = pl.pallas_call(
        kernel,
        out_shape=jax.ShapeDtypeStruct((ROWS, 1, COLS), f32),
        in_specs=[hbm, hbm, smem, smem, smem],
        out_specs=pl.BlockSpec(memory_space=pltpu.VMEM),
        scratch_shapes=[
            pltpu.VMEM((8 * ROWS * TILES, LANES), f32),
            pltpu.VMEM((8, 2, PIECE, COLS), f32),
            pltpu.VMEM((8 * ROWS, COLS), f32),
            pltpu.VMEM((7, SLOT, COLS), f32),
            pltpu.VMEM((7, SLOT, COLS), f32),
            pltpu.VMEM((SLOT, COLS), f32),
            pltpu.VMEM((SLOT, COLS), f32),
            pltpu.VMEM((SLOT, COLS), f32),
            pltpu.VMEM((COLS, COLS), jnp.bfloat16),
            dma((5,)), dma((5,)),
            dma((2, 4, 4)), dma((2, 4, 4)),
            dma((8, 4)), dma((8, 4)),
            dma((7,)), dma((7,)), dma((1,)),
            dma((8,)), dma((8,)),
            dma((8,)), dma((8,)),
        ],
        compiler_params=pltpu.CompilerParams(
            collective_id=0, has_side_effects=True, vmem_limit_bytes=56 * 2**20
        ),
        name="ladder",
    )(tiles, amplitudes, block_map, eps_vir, eps_occ)
    return jnp.transpose(update.reshape(1, ROWS, 1, COLS), (0, 2, 1, 3))


def solution(mesh):
    in_specs = (P("blk", "pair", None, None), P("blk", None), P("blk", "pair", None), P(), P())
    out_specs = P("blk", "pair", None, None)
    return jax.shard_map(body, mesh=mesh, in_specs=in_specs, out_specs=out_specs, check_vma=False)
```

```python
import functools

import jax
import jax.numpy as jnp
from jax import lax
from jax.experimental import pallas as pl
from jax.experimental.pallas import tpu as pltpu
from jax.sharding import PartitionSpec as P

MESH = pl.DeviceIdType.MESH

OCCUPIED = 16
SIDE = 5
ROWS = 25
SLOT = 32
COLS = 256
LANES = 128
TILES = 25
LAYERS = 8
PIECE = 192
PART = 64
X, Y, Z = 4, 8, 8
SENDS = ((2, 1, 0), (6, -1, 0), (3, 0, 1), (5, 0, -1), (1, -1, 1), (7, 1, -1), (4, 2, 0))
RETURNS = (6, 4, 5, 0, 1, 2, 3)
PLACES = (0, -1, -2, -3, 1, 2, 3, 4)


def device(z, y, x, core):
    return (z * 2 + y // 4, (y % 4) * 8 + x * 2 + core)


def share(layer, colour):
    low = 2 - (layer + colour) % 2
    start_low = 3 * (colour // 2) + (colour % 2) * (3 - low)
    start_high = 3 * (colour // 2) + (colour % 2) * low
    return low, start_low, start_high


def tile_places(parity):
    places = {}
    for colour in range(8):
        low, start_low, start_high = share(parity, colour)
        for i in range(low):
            places[start_low + i] = (colour, i)
        for i in range(3 - low):
            places[13 + start_high + i] = (colour, low + i)
    return places


def kernel(
    v_ref, t_ref, map_hbm, vir_hbm, occ_hbm, out_ref,
    map_ref, vir_ref, occ_ref, small,
    raw, packed, vbuf, tbuf, tlast, acc, give, parts, mine, other, den, turn,
    ready, raw_sem, tin_send, tin_recv, ring_send, ring_recv, core_send, core_recv,
    last_send, last_recv, last_across,
    v_send, v_recv, v_own, part_send, part_recv, mir_send, mir_recv,
):
    blk, pair = lax.axis_index("blk"), lax.axis_index("pair")
    z, y_hi = blk // 2, blk % 2
    y_lo, x, core = pair // 8, (pair // 2) % 4, pair % 2
    y = y_hi * 4 + y_lo
    colour = (3 * y + 2 * x) % 8
    partner_colour = (3 * (7 - y) + 2 * x) % 8

    def at(dx=0, dy=0, dz=0):
        return device((z + dz + Z) % Z, (y + dy + Y) % Y, (x + dx + X) % X, core)

    sibling = device(z, y, x, 1 - core)
    up, down = at(dz=1), at(dz=-1)
    twin = at(dy=2 - 4 * (y_lo // 2))
    partner = device(z, 7 - y, x, core)

    load = pltpu.make_async_copy(v_ref, raw.reshape(ROWS, LAYERS * TILES, 1, LANES), raw_sem.at[0])
    load.start()
    tables = [
        pltpu.make_async_copy(src, dst, small.at[n])
        for n, (src, dst) in enumerate(((map_hbm, map_ref), (vir_hbm, vir_ref), (occ_hbm, occ_ref)))
    ]
    for copy in tables:
        copy.start()

    barrier = pltpu.get_barrier_semaphore()
    greet = [sibling, twin, partner] + [at(dx=-dx, dy=-dy) for _, dx, dy in SENDS]

    def signal(semaphore, peer):
        pl.semaphore_signal(semaphore, inc=1, device_id=peer, device_id_type=MESH)

    for peer in greet:
        signal(barrier, peer)
    pl.when(z < Z - 1)(lambda: signal(barrier, up))
    pl.when(z == 0)(lambda: signal(barrier, down))
    load.wait()

    def pack(pairs, carry):
        for parity in range(2):
            layer = 2 * pairs + parity
            for tile, (of_colour, place) in sorted(tile_places(parity).items()):
                value = raw[pl.ds(TILES * layer + tile, ROWS, stride=LAYERS * TILES), :]
                packed[pl.ds(of_colour * ROWS * TILES + 3 * layer + place, ROWS, stride=TILES), :] = value
            value = raw[pl.ds(TILES * layer + 12, ROWS, stride=LAYERS * TILES), :]
            packed[pl.ds(layer * ROWS * TILES + 24, ROWS, stride=TILES), :] = value
        return carry

    lax.fori_loop(0, LAYERS // 2, pack, 0)

    lower = (z + Z - 1) // Z + z // (Z - 1)
    pl.semaphore_wait(barrier, len(greet) + lower)
    pl.when(z > 0)(lambda: signal(ready.at[0], down))
    pl.when(z == Z - 1)(lambda: signal(ready.at[1], up))

    started = []

    def remote(src, dst, send, recv, peer):
        return pltpu.make_async_remote_copy(
            src_ref=src, dst_ref=dst, send_sem=send, recv_sem=recv, device_id=peer, device_id_type=MESH
        )

    def go(copy):
        copy.start()
        started.append(copy)

    def landed(ref, sem):
        pltpu.make_async_copy(ref, ref, sem).wait()

    def held(of_colour):
        low, start_low, start_high = share(z, of_colour)
        always = (1 - y_hi) * 128 * start_low + y_hi * (64 + 128 * (start_high + 2 - low))
        middle = (1 - y_hi) * 128 * (start_low + 1) + y_hi * (64 + 128 * start_high)
        rows = [t_ref.at[pl.ds(pl.multiple_of(first + PART * core, PART), PART)] for first in (always, middle)]
        return rows, low + y_hi == 2

    def tile_rows(layer, tile):
        k = (2 * y_hi, 1, 2 - 2 * y_hi)[tile]
        return tbuf.at[layer, core, pl.ds(pl.multiple_of(PART * k, PART), PART)]

    own_rows, own_middle = held(colour)
    out_rows, out_middle = held(partner_colour)
    partner_part = tile_rows(z, 0)
    middle_out = remote(out_rows[1], tile_rows(z, 1), tin_send.at[1], tin_recv.at[1], partner)
    first_up = remote(own_rows[0], tile_rows(z, 0), ring_send.at[0, 0, 0], ring_recv.at[0, 0, 0], up)
    first_down = remote(own_rows[0], tile_rows(z, 0), ring_send.at[1, 0, 0], ring_recv.at[1, 0, 0], down)
    pl.when(z > 0)(first_down.start)
    pl.when(z == Z - 1)(first_up.start)
    go(remote(out_rows[0], partner_part, tin_send.at[2], tin_recv.at[2], partner))
    pl.when(out_middle)(middle_out.start)
    native = pltpu.make_async_copy(own_rows[0], tile_rows(z, 0), tin_recv.at[0])
    native.start()
    pl.when(own_middle)(pltpu.make_async_copy(own_rows[1], tile_rows(z, 1), tin_recv.at[1]).start)

    ahead = (z - colour + Z) % Z
    last = tlast.at[pl.ds(pl.multiple_of(PART * core, PART), PART)]
    last_rows = t_ref.at[pl.ds(pl.multiple_of((1 - core) * 1536, PART), PART)]
    last_out = remote(last_rows, last, last_send.at[2], last_recv.at[0], partner)
    sends_last = (partner_colour == z) & (y_hi == core)
    pl.when(sends_last)(last_out.start)
    pl.when((ahead == 0) & (y_hi == core))(pltpu.make_async_copy(last_rows, last, last_recv.at[0]).start)
    last_up = remote(last, last, last_send.at[0], last_recv.at[0], up)
    last_down = remote(last, last, last_send.at[1], last_recv.at[0], down)
    last_over = remote(last, last, last_send.at[3], last_across.at[0], sibling)

    def pass_last(hop):
        if hop == 0:
            @pl.when(ahead == 0)
            def _():
                landed(last, last_recv.at[0])
                last_up.start()
                last_down.start()
                last_over.start()
            return

        if hop < 4:
            @pl.when(ahead == hop)
            def _():
                landed(last, last_recv.at[0])
                if hop < 3:
                    last_up.start()
                last_over.start()

        @pl.when(ahead == Z - hop)
        def _():
            landed(last, last_recv.at[0])
            if hop < 4:
                last_down.start()
            last_over.start()

    slots = vbuf.reshape(8, ROWS, TILES, 1, LANES)
    sorted_v = packed.reshape(8, ROWS, TILES, 1, LANES)
    vout = []
    for i, (step, dx, dy) in enumerate(SENDS):
        src = sorted_v.at[(colour + step) % 8]
        vout.append(remote(src, slots.at[i + 1], v_send.at[i], v_recv.at[i], at(dx=dx, dy=dy)))
        vout[-1].start()
    own = pltpu.make_async_copy(sorted_v.at[colour], slots.at[0], v_own.at[0])
    own.start()

    for copy in tables:
        copy.wait()
    lane = lax.broadcasted_iota(jnp.int32, (1, COLS), 1)
    occ_i = jnp.zeros((1, COLS), jnp.float32)
    occ_j = jnp.zeros((1, COLS), jnp.float32)
    for i in range(OCCUPIED):
        occ_i = jnp.where((lane >> 4) == i, occ_ref[i], occ_i)
        occ_j = jnp.where((lane & 15) == i, occ_ref[i], occ_j)
    for s in range(SIDE):
        for t in range(SIDE):
            both = vir_ref[map_ref[0, 0, 0] * SIDE + s] + vir_ref[map_ref[0, 0, 1] * SIDE + t]
            r = s * SIDE + t
            den[r : r + 1, :] = (both - occ_i) - occ_j
    row = lax.broadcasted_iota(jnp.int32, (COLS, COLS), 0)
    col = lax.broadcasted_iota(jnp.int32, (COLS, COLS), 1)
    turn[...] = (((row >> 4) == (col & 15)) & ((row & 15) == (col >> 4))).astype(jnp.bfloat16)

    def layer_of(place):
        return (z + PLACES[place] + Z) % Z

    def ring(way, hop, role):
        ref = tile_rows((z - hop + Z) % Z if way == 0 else (z + hop) % Z, role)
        return remote(ref, ref, ring_send.at[way, hop, role], ring_recv.at[way, hop, role], up if way == 0 else down)

    def arrived(way, hop, role):
        landed(tile_rows(layer_of(hop + 1 + 3 * way if hop < 3 else 7), role), ring_recv.at[way, hop, role])

    def across(place):
        ref = tbuf.at[layer_of(place), core]
        return remote(ref, ref, core_send.at[place], core_recv.at[place], sibling)

    @pl.when(z < Z - 1)
    def _():
        pl.semaphore_wait(ready.at[0], 1)
        first_up.start()

    for role in (2, 1):
        landed(tile_rows(z, role), tin_recv.at[role])
        go(ring(0, 0, role))

    @pl.when(z == 0)
    def _():
        pl.semaphore_wait(ready.at[1], 1)
        first_down.start()

    for role in (2, 1):
        go(ring(1, 0, role))
    native.wait()
    go(across(0))
    pass_last(0)
    for hop in range(1, 3):
        for role in (0, 2, 1):
            for way in (1, 0):
                arrived(way, hop - 1, role)
                go(ring(way, hop, role))
        for way in (1, 0):
            go(across(hop + 3 * way))
        pass_last(hop)
    for role in (0, 2, 1):
        arrived(1, 2, role)
        go(ring(1, 3, role))
    go(across(6))

    own.wait()
    for copy in vout:
        copy.wait_recv()

    def split(value):
        high = value.astype(jnp.bfloat16)
        return high, (value - high.astype(jnp.float32)).astype(jnp.bfloat16)

    def product(v, t):
        v_high, v_low = split(v)
        t_high, t_low = split(t)
        dot = functools.partial(jnp.dot, preferred_element_type=jnp.float32)
        return dot(v_high, t_high) + (dot(v_low, t_high) + dot(v_high, t_low))

    def gathered(tile, tiles):
        return jnp.concatenate([vbuf[pl.ds(tile + k, 8 * ROWS, stride=TILES), :] for k in range(tiles)], axis=1)

    def add(place):
        layer = layer_of(place)
        landed(tbuf.at[layer, 1 - core], core_recv.at[place])
        t = [tbuf[layer, c, PART * k : PART * (k + 1), :] for k in range(3) for c in range(2)]
        term = product(gathered(3 * layer, 3), jnp.concatenate(t, axis=0))
        if place == 0:
            acc[...] = term
        else:
            acc[...] += term

    for place in (0, 4, 1, 5, 2):
        add(place)
    for role in (0, 2, 1):
        arrived(0, 2, role)
    go(across(3))
    pass_last(3)
    for role in (0, 2, 1):
        arrived(1, 3, role)
    go(across(7))
    pass_last(4)
    for place in (6, 3, 7):
        add(place)
    landed(tlast.at[pl.ds(pl.multiple_of(PART * (1 - core), PART), PART)], last_across.at[0])
    final = acc[...] + product(gathered(24, 1), tlast[...])

    back = []
    for i in RETURNS:
        _, dx, dy = SENDS[i]
        give[i, 0:ROWS, :] = final[ROWS * (i + 1) : ROWS * (i + 2), :]
        copy = remote(give.at[i], parts.at[i], part_send.at[i], part_recv.at[i], at(dx=-dx, dy=-dy))
        copy.start()
        back.append(copy)

    for copy in vout + started:
        copy.wait_send()
    pl.when(out_middle)(middle_out.wait_send)
    pl.when(sends_last)(last_out.wait_send)
    pl.when(ahead < 3)(last_up.wait_send)
    pl.when((ahead == 0) | (ahead > 4))(last_down.wait_send)
    first_up.wait_send()
    first_down.wait_send()
    last_over.wait_send()
    total = final[0:SLOT, :]
    for i in range(7):
        back[i].wait_recv()
        total = total + parts[RETURNS[i]]
    mine[...] = total
    swap = remote(mine, other, mir_send.at[0], mir_recv.at[0], twin)
    swap.start()
    for copy in back:
        copy.wait_send()
    swap.wait_recv()
    dot = functools.partial(jnp.dot, preferred_element_type=jnp.float32)
    high, rest = split(other[...])
    mid = (other[...] - high.astype(jnp.float32)) - rest.astype(jnp.float32)
    turned = (dot(high, turn[...]) + dot(rest, turn[...])) + dot(mid.astype(jnp.bfloat16), turn[...])
    for s in range(SIDE):
        for t in range(SIDE):
            r, q = s * SIDE + t, t * SIDE + s
            out_ref[r] = (total[r : r + 1] + turned[q : q + 1]) / den[r : r + 1, :]

    swap.wait_send()


def body(integrals, amplitudes, block_map, eps_vir, eps_occ):
    hbm = pl.BlockSpec(memory_space=pltpu.HBM)
    dma = pltpu.SemaphoreType.DMA
    f32 = jnp.float32
    tiles = jnp.transpose(integrals, (0, 2, 1, 3)).reshape(ROWS, 8 * TILES, 1, LANES)
    update = pl.pallas_call(
        kernel,
        out_shape=jax.ShapeDtypeStruct((ROWS, 1, COLS), f32),
        in_specs=[hbm] * 5,
        out_specs=pl.BlockSpec(memory_space=pltpu.VMEM),
        scratch_shapes=[
            pltpu.SMEM((1, 1, 2), jnp.int32),
            pltpu.SMEM((160,), f32),
            pltpu.SMEM((16,), f32),
            dma((3,)),
            pltpu.VMEM((8 * ROWS * TILES, LANES), f32),
            pltpu.VMEM((8 * ROWS * TILES, LANES), f32),
            pltpu.VMEM((8 * ROWS * TILES, LANES), f32),
            pltpu.VMEM((LAYERS, 2, PIECE, COLS), f32),
            pltpu.VMEM((128, COLS), f32),
            pltpu.VMEM((8 * ROWS, COLS), f32),
            pltpu.VMEM((7, SLOT, COLS), f32),
            pltpu.VMEM((7, SLOT, COLS), f32),
            pltpu.VMEM((SLOT, COLS), f32),
            pltpu.VMEM((SLOT, COLS), f32),
            pltpu.VMEM((SLOT, COLS), f32),
            pltpu.VMEM((COLS, COLS), jnp.bfloat16),
            pltpu.SemaphoreType.REGULAR((2,)),
            dma((1,)), dma((3,)), dma((3,)),
            dma((2, 4, 3)), dma((2, 4, 3)),
            dma((8,)), dma((8,)),
            dma((4,)), dma((1,)), dma((1,)),
            dma((7,)), dma((7,)), dma((1,)),
            dma((8,)), dma((8,)),
            dma((8,)), dma((8,)),
        ],
        compiler_params=pltpu.CompilerParams(
            collective_id=0, has_side_effects=True, vmem_limit_bytes=56 * 2**20
        ),
        name="ladder",
    )(tiles, amplitudes, block_map, eps_vir, eps_occ)
    return jnp.transpose(update.reshape(1, ROWS, 1, COLS), (0, 2, 1, 3))


def solution(mesh):
    in_specs = (P("blk", "pair", None, None), P("blk", None), P("blk", "pair", None), P(), P())
    out_specs = P("blk", "pair", None, None)
    return jax.shard_map(body, mesh=mesh, in_specs=in_specs, out_specs=out_specs, check_vma=False)
```

```python
import functools

import jax
import jax.numpy as jnp
from jax import lax
from jax.experimental import pallas as pl
from jax.experimental.pallas import tpu as pltpu
from jax.sharding import PartitionSpec as P

MESH = pl.DeviceIdType.MESH

OCCUPIED = 16
SIDE = 5
ROWS = 25
SLOT = 32
COLS = 256
LANES = 128
TILES = 25
LAYERS = 8
PIECE = 192
PART = 64
X, Y, Z = 4, 8, 8
SENDS = ((2, 1, 0), (6, -1, 0), (3, 0, 1), (5, 0, -1), (1, -1, 1), (7, 1, -1), (4, 2, 0))
RETURNS = (6, 4, 5, 0, 1, 2, 3)
PLACES = (0, -1, -2, -3, 1, 2, 3, 4)


def device(z, y, x, core):
    return (z * 2 + y // 4, (y % 4) * 8 + x * 2 + core)


def share(layer, colour):
    low = 2 - (layer + colour) % 2
    start_low = 3 * (colour // 2) + (colour % 2) * (3 - low)
    start_high = 3 * (colour // 2) + (colour % 2) * low
    return low, start_low, start_high


def tile_places(parity):
    places = {}
    for colour in range(8):
        low, start_low, start_high = share(parity, colour)
        for i in range(low):
            places[start_low + i] = (colour, i)
        for i in range(3 - low):
            places[13 + start_high + i] = (colour, low + i)
    return places


def kernel(
    v_ref, t_ref, map_hbm, vir_hbm, occ_hbm, out_ref,
    map_ref, vir_ref, occ_ref, small,
    raw, packed, vbuf, tbuf, tlast, acc, give, parts, mine, other, den, turn,
    ready, raw_sem, tin_send, tin_recv, ring_send, ring_recv, core_send, core_recv,
    last_send, last_recv, last_across,
    v_send, v_recv, v_own, part_send, part_recv, mir_send, mir_recv,
):
    blk, pair = lax.axis_index("blk"), lax.axis_index("pair")
    z, y_hi = blk // 2, blk % 2
    y_lo, x, core = pair // 8, (pair // 2) % 4, pair % 2
    y = y_hi * 4 + y_lo
    colour = (3 * y + 2 * x) % 8
    partner_colour = (3 * (7 - y) + 2 * x) % 8

    def at(dx=0, dy=0, dz=0):
        return device((z + dz + Z) % Z, (y + dy + Y) % Y, (x + dx + X) % X, core)

    sibling = device(z, y, x, 1 - core)
    up, down = at(dz=1), at(dz=-1)
    twin = at(dy=2 - 4 * (y_lo // 2))
    partner = device(z, 7 - y, x, core)

    load = pltpu.make_async_copy(v_ref, raw.reshape(ROWS, LAYERS * TILES, 1, LANES), raw_sem.at[0])
    load.start()
    tables = [
        pltpu.make_async_copy(src, dst, small.at[n])
        for n, (src, dst) in enumerate(((map_hbm, map_ref), (vir_hbm, vir_ref), (occ_hbm, occ_ref)))
    ]
    for copy in tables:
        copy.start()

    barrier = pltpu.get_barrier_semaphore()
    greet = [sibling, twin, partner] + [at(dx=-dx, dy=-dy) for _, dx, dy in SENDS]

    def signal(semaphore, peer):
        pl.semaphore_signal(semaphore, inc=1, device_id=peer, device_id_type=MESH)

    for peer in greet:
        signal(barrier, peer)
    pl.when(z < Z - 1)(lambda: signal(barrier, up))
    pl.when(z == 0)(lambda: signal(barrier, down))
    lower = (z + Z - 1) // Z + z // (Z - 1)
    pl.semaphore_wait(barrier, len(greet) + lower)
    pl.when(z > 0)(lambda: signal(ready.at[0], down))
    pl.when(z == Z - 1)(lambda: signal(ready.at[1], up))

    started = []

    def remote(src, dst, send, recv, peer):
        return pltpu.make_async_remote_copy(
            src_ref=src, dst_ref=dst, send_sem=send, recv_sem=recv, device_id=peer, device_id_type=MESH
        )

    def go(copy):
        copy.start()
        started.append(copy)

    def landed(ref, sem):
        pltpu.make_async_copy(ref, ref, sem).wait()

    def held(of_colour):
        low, start_low, start_high = share(z, of_colour)
        always = (1 - y_hi) * 128 * start_low + y_hi * (64 + 128 * (start_high + 2 - low))
        middle = (1 - y_hi) * 128 * (start_low + low - 1) + y_hi * (64 + 128 * start_high)
        rows = [t_ref.at[pl.ds(pl.multiple_of(first + PART * core, PART), PART)] for first in (always, middle)]
        return rows, low + y_hi == 2

    def tile_rows(layer, tile):
        k = (2 * y_hi, 1, 2 - 2 * y_hi)[tile]
        return tbuf.at[layer, core, pl.ds(pl.multiple_of(PART * k, PART), PART)]

    own_rows, own_middle = held(colour)
    out_rows, out_middle = held(partner_colour)
    partner_part = tile_rows(z, 0)
    middle_out = remote(out_rows[1], tile_rows(z, 1), tin_send.at[1], tin_recv.at[1], partner)
    first_up = remote(own_rows[0], tile_rows(z, 0), ring_send.at[0, 0, 0], ring_recv.at[0, 0, 0], up)
    first_down = remote(own_rows[0], tile_rows(z, 0), ring_send.at[1, 0, 0], ring_recv.at[1, 0, 0], down)
    pl.when(z > 0)(first_down.start)
    pl.when(z == Z - 1)(first_up.start)
    go(remote(out_rows[0], partner_part, tin_send.at[2], tin_recv.at[2], partner))
    pl.when(out_middle)(middle_out.start)
    native = pltpu.make_async_copy(own_rows[0], tile_rows(z, 0), tin_recv.at[0])
    native.start()
    pl.when(own_middle)(pltpu.make_async_copy(own_rows[1], tile_rows(z, 1), tin_recv.at[1]).start)

    ahead = (z - colour + Z) % Z
    last = tlast.at[pl.ds(pl.multiple_of(PART * core, PART), PART)]
    last_rows = t_ref.at[pl.ds(pl.multiple_of((1 - core) * 1536, PART), PART)]
    last_out = remote(last_rows, last, last_send.at[2], last_recv.at[0], partner)
    sends_last = (partner_colour == z) & (y_hi == core)
    pl.when(sends_last)(last_out.start)
    pl.when((ahead == 0) & (y_hi == core))(pltpu.make_async_copy(last_rows, last, last_recv.at[0]).start)
    last_up = remote(last, last, last_send.at[0], last_recv.at[0], up)
    last_down = remote(last, last, last_send.at[1], last_recv.at[0], down)
    last_over = remote(last, last, last_send.at[3], last_across.at[0], sibling)

    def pass_last(hop):
        if hop == 0:
            @pl.when(ahead == 0)
            def _():
                landed(last, last_recv.at[0])
                last_up.start()
                last_down.start()
                last_over.start()
            return

        if hop < 4:
            @pl.when(ahead == hop)
            def _():
                landed(last, last_recv.at[0])
                if hop < 3:
                    last_up.start()
                last_over.start()

        @pl.when(ahead == Z - hop)
        def _():
            landed(last, last_recv.at[0])
            if hop < 4:
                last_down.start()
            last_over.start()

    load.wait()

    def pack(pairs, carry):
        for parity in range(2):
            layer = 2 * pairs + parity
            for tile, (of_colour, place) in sorted(tile_places(parity).items()):
                value = raw[pl.ds(TILES * layer + tile, ROWS, stride=LAYERS * TILES), :]
                packed[pl.ds(of_colour * ROWS * TILES + 3 * layer + place, ROWS, stride=TILES), :] = value
            value = raw[pl.ds(TILES * layer + 12, ROWS, stride=LAYERS * TILES), :]
            packed[pl.ds(layer * ROWS * TILES + 24, ROWS, stride=TILES), :] = value
        return carry

    lax.fori_loop(0, LAYERS // 2, pack, 0)

    slots = vbuf.reshape(8, ROWS, TILES, 1, LANES)
    sorted_v = packed.reshape(8, ROWS, TILES, 1, LANES)
    vout = []
    for i in RETURNS:
        step, dx, dy = SENDS[i]
        src = sorted_v.at[(colour + step) % 8]
        vout.append(remote(src, slots.at[i + 1], v_send.at[i], v_recv.at[i], at(dx=dx, dy=dy)))
        vout[-1].start()
    own = pltpu.make_async_copy(sorted_v.at[colour], slots.at[0], v_own.at[0])
    own.start()

    def layer_of(place):
        return (z + PLACES[place] + Z) % Z

    def ring(way, hop, role):
        ref = tile_rows((z - hop + Z) % Z if way == 0 else (z + hop) % Z, role)
        return remote(ref, ref, ring_send.at[way, hop, role], ring_recv.at[way, hop, role], up if way == 0 else down)

    def arrived(way, hop, role):
        landed(tile_rows(layer_of(hop + 1 + 3 * way if hop < 3 else 7), role), ring_recv.at[way, hop, role])

    def across(place):
        ref = tbuf.at[layer_of(place), core]
        return remote(ref, ref, core_send.at[place], core_recv.at[place], sibling)

    @pl.when(z < Z - 1)
    def _():
        pl.semaphore_wait(ready.at[0], 1)
        first_up.start()

    for role in (2, 1):
        landed(tile_rows(z, role), tin_recv.at[role])
        go(ring(0, 0, role))

    @pl.when(z == 0)
    def _():
        pl.semaphore_wait(ready.at[1], 1)
        first_down.start()

    for role in (2, 1):
        go(ring(1, 0, role))
    native.wait()
    go(across(0))
    pass_last(0)
    for hop in range(1, 3):
        for role in (0, 2, 1):
            for way in (1, 0):
                arrived(way, hop - 1, role)
                go(ring(way, hop, role))
        for way in (1, 0):
            go(across(hop + 3 * way))
        pass_last(hop)
    for role in (0, 2, 1):
        arrived(1, 2, role)
        go(ring(1, 3, role))
    go(across(6))

    own.wait()
    for copy in vout:
        copy.wait_recv()

    def split(value):
        high = value.astype(jnp.bfloat16)
        return high, (value - high.astype(jnp.float32)).astype(jnp.bfloat16)

    def product(v, t):
        v_high, v_low = split(v)
        t_high, t_low = split(t)
        dot = functools.partial(jnp.dot, preferred_element_type=jnp.float32)
        return dot(v_high, t_high) + (dot(v_low, t_high) + dot(v_high, t_low))

    def gathered(tile, tiles):
        return jnp.concatenate([vbuf[pl.ds(tile + k, 8 * ROWS, stride=TILES), :] for k in range(tiles)], axis=1)

    def add(place):
        layer = layer_of(place)
        landed(tbuf.at[layer, 1 - core], core_recv.at[place])
        t = [tbuf[layer, c, PART * k : PART * (k + 1), :] for k in range(3) for c in range(2)]
        term = product(gathered(3 * layer, 3), jnp.concatenate(t, axis=0))
        if place == 0:
            acc[...] = term
        else:
            acc[...] += term

    for place in (0, 4, 1, 5, 2):
        add(place)
    for role in (0, 2, 1):
        arrived(0, 2, role)
    go(across(3))
    pass_last(3)
    for role in (0, 2, 1):
        arrived(1, 3, role)
    go(across(7))
    pass_last(4)
    for place in (6, 3, 7):
        add(place)
    landed(tlast.at[pl.ds(pl.multiple_of(PART * (1 - core), PART), PART)], last_across.at[0])
    final = acc[...] + product(gathered(24, 1), tlast[...])

    back = []
    give_rows = give.reshape(7, ROWS, 2, 1, LANES)
    part_rows = parts.reshape(7, ROWS, 2, 1, LANES)
    for i in RETURNS:
        _, dx, dy = SENDS[i]
        for half in range(2):
            value = final[ROWS * (i + 1) : ROWS * (i + 2), LANES * half : LANES * (half + 1)]
            give[pl.ds(2 * ROWS * i + half, ROWS, stride=2), :] = value
        copy = remote(give_rows.at[i], part_rows.at[i], part_send.at[i], part_recv.at[i], at(dx=-dx, dy=-dy))
        copy.start()
        back.append(copy)

    for copy in tables:
        copy.wait()
    lane = lax.broadcasted_iota(jnp.int32, (1, COLS), 1)
    occ_i = jnp.zeros((1, COLS), jnp.float32)
    occ_j = jnp.zeros((1, COLS), jnp.float32)
    for i in range(OCCUPIED):
        occ_i = jnp.where((lane >> 4) == i, occ_ref[i], occ_i)
        occ_j = jnp.where((lane & 15) == i, occ_ref[i], occ_j)
    for s in range(SIDE):
        for t in range(SIDE):
            both = vir_ref[map_ref[0, 0, 0] * SIDE + s] + vir_ref[map_ref[0, 0, 1] * SIDE + t]
            r = s * SIDE + t
            den[r : r + 1, :] = (both - occ_i) - occ_j
    row = lax.broadcasted_iota(jnp.int32, (COLS, COLS), 0)
    col = lax.broadcasted_iota(jnp.int32, (COLS, COLS), 1)
    turn[...] = (((row >> 4) == (col & 15)) & ((row & 15) == (col >> 4))).astype(jnp.bfloat16)

    for copy in vout + started:
        copy.wait_send()
    pl.when(out_middle)(middle_out.wait_send)
    pl.when(sends_last)(last_out.wait_send)
    pl.when(ahead < 3)(last_up.wait_send)
    pl.when((ahead == 0) | (ahead > 4))(last_down.wait_send)
    first_up.wait_send()
    first_down.wait_send()
    last_over.wait_send()
    total = final[0:ROWS, :]
    for i in range(7):
        back[i].wait_recv()
        n = 2 * ROWS * RETURNS[i]
        halves = [parts[pl.ds(n + half, ROWS, stride=2), :] for half in range(2)]
        total = total + jnp.concatenate(halves, axis=1)
    mine[0:ROWS, :] = total
    swap = remote(mine, other, mir_send.at[0], mir_recv.at[0], twin)
    swap.start()
    for copy in back:
        copy.wait_send()
    swap.wait_recv()
    dot = functools.partial(jnp.dot, preferred_element_type=jnp.float32)
    high, rest = split(other[...])
    mid = (other[...] - high.astype(jnp.float32)) - rest.astype(jnp.float32)
    turned = (dot(high, turn[...]) + dot(rest, turn[...])) + dot(mid.astype(jnp.bfloat16), turn[...])
    for s in range(SIDE):
        for t in range(SIDE):
            r, q = s * SIDE + t, t * SIDE + s
            out_ref[r] = (total[r : r + 1] + turned[q : q + 1]) / den[r : r + 1, :]

    swap.wait_send()


def body(integrals, amplitudes, block_map, eps_vir, eps_occ):
    hbm = pl.BlockSpec(memory_space=pltpu.HBM)
    dma = pltpu.SemaphoreType.DMA
    f32 = jnp.float32
    tiles = jnp.transpose(integrals, (0, 2, 1, 3)).reshape(ROWS, 8 * TILES, 1, LANES)
    update = pl.pallas_call(
        kernel,
        out_shape=jax.ShapeDtypeStruct((ROWS, 1, COLS), f32),
        in_specs=[hbm] * 5,
        out_specs=pl.BlockSpec(memory_space=pltpu.VMEM),
        scratch_shapes=[
            pltpu.SMEM((1, 1, 2), jnp.int32),
            pltpu.SMEM((160,), f32),
            pltpu.SMEM((16,), f32),
            dma((3,)),
            pltpu.VMEM((8 * ROWS * TILES, LANES), f32),
            pltpu.VMEM((8 * ROWS * TILES, LANES), f32),
            pltpu.VMEM((8 * ROWS * TILES, LANES), f32),
            pltpu.VMEM((LAYERS, 2, PIECE, COLS), f32),
            pltpu.VMEM((128, COLS), f32),
            pltpu.VMEM((8 * ROWS, COLS), f32),
            pltpu.VMEM((7 * ROWS * 2, LANES), f32),
            pltpu.VMEM((7 * ROWS * 2, LANES), f32),
            pltpu.VMEM((SLOT, COLS), f32),
            pltpu.VMEM((SLOT, COLS), f32),
            pltpu.VMEM((SLOT, COLS), f32),
            pltpu.VMEM((COLS, COLS), jnp.bfloat16),
            pltpu.SemaphoreType.REGULAR((2,)),
            dma((1,)), dma((3,)), dma((3,)),
            dma((2, 4, 3)), dma((2, 4, 3)),
            dma((8,)), dma((8,)),
            dma((4,)), dma((1,)), dma((1,)),
            dma((7,)), dma((7,)), dma((1,)),
            dma((8,)), dma((8,)),
            dma((8,)), dma((8,)),
        ],
        compiler_params=pltpu.CompilerParams(
            collective_id=0, has_side_effects=True, vmem_limit_bytes=56 * 2**20
        ),
        name="ladder",
    )(tiles, amplitudes, block_map, eps_vir, eps_occ)
    return jnp.transpose(update.reshape(1, ROWS, 1, COLS), (0, 2, 1, 3))


def solution(mesh):
    in_specs = (P("blk", "pair", None, None), P("blk", None), P("blk", "pair", None), P(), P())
    out_specs = P("blk", "pair", None, None)
    return jax.shard_map(body, mesh=mesh, in_specs=in_specs, out_specs=out_specs, check_vma=False)
```

```python
import functools

import jax
import jax.numpy as jnp
from jax import lax
from jax.experimental import pallas as pl
from jax.experimental.pallas import tpu as pltpu
from jax.sharding import PartitionSpec as P

MESH = pl.DeviceIdType.MESH

OCCUPIED = 16
SIDE = 5
ROWS = 25
SLOT = 32
COLS = 256
LANES = 128
TILES = 25
LAYERS = 8
PIECE = 192
PART = 64
X, Y, Z = 4, 8, 8
SENDS = ((2, 1, 0), (6, -1, 0), (3, 0, 1), (5, 0, -1), (1, -1, 1), (7, 1, -1), (4, 2, 0))
RETURNS = (6, 4, 5, 0, 1, 2, 3)
PLACES = (0, -1, -2, -3, 1, 2, 3, 4)


def device(z, y, x, core):
    return (z * 2 + y // 4, (y % 4) * 8 + x * 2 + core)


def share(layer, colour):
    low = 2 - (layer + colour) % 2
    start_low = 3 * (colour // 2) + (colour % 2) * (3 - low)
    start_high = 3 * (colour // 2) + (colour % 2) * low
    return low, start_low, start_high


def tile_places(parity):
    places = {}
    for colour in range(8):
        low, start_low, start_high = share(parity, colour)
        for i in range(low):
            places[start_low + i] = (colour, i)
        for i in range(3 - low):
            places[13 + start_high + i] = (colour, low + i)
    return places


def kernel(
    v_ref, t_ref, map_hbm, vir_hbm, occ_hbm, out_ref,
    map_ref, vir_ref, occ_ref, small,
    raw, packed, vbuf, tbuf, tlast, acc, give, parts, mine, other, den, turn,
    ready, raw_sem, tin_send, tin_recv, ring_send, ring_recv, core_send, core_recv,
    last_send, last_recv, last_across,
    v_send, v_recv, v_own, part_send, part_recv, mir_send, mir_recv,
):
    blk, pair = lax.axis_index("blk"), lax.axis_index("pair")
    z, y_hi = blk // 2, blk % 2
    y_lo, x, core = pair // 8, (pair // 2) % 4, pair % 2
    y = y_hi * 4 + y_lo
    colour = (3 * y + 2 * x) % 8
    partner_colour = (3 * (7 - y) + 2 * x) % 8

    def at(dx=0, dy=0, dz=0):
        return device((z + dz + Z) % Z, (y + dy + Y) % Y, (x + dx + X) % X, core)

    sibling = device(z, y, x, 1 - core)
    up, down = at(dz=1), at(dz=-1)
    twin = at(dy=2 - 4 * (y_lo // 2))
    partner = device(z, 7 - y, x, core)

    load = pltpu.make_async_copy(v_ref, raw.reshape(ROWS, LAYERS * TILES, 1, LANES), raw_sem.at[0])
    load.start()
    tables = [
        pltpu.make_async_copy(src, dst, small.at[n])
        for n, (src, dst) in enumerate(((map_hbm, map_ref), (vir_hbm, vir_ref), (occ_hbm, occ_ref)))
    ]
    for copy in tables:
        copy.start()

    barrier = pltpu.get_barrier_semaphore()
    greet = [sibling, twin, partner] + [at(dx=-dx, dy=-dy) for _, dx, dy in SENDS]

    def signal(semaphore, peer):
        pl.semaphore_signal(semaphore, inc=1, device_id=peer, device_id_type=MESH)

    for peer in greet:
        signal(barrier, peer)
    pl.when(z < Z - 1)(lambda: signal(barrier, up))
    pl.when(z == 0)(lambda: signal(barrier, down))
    lower = (z + Z - 1) // Z + z // (Z - 1)
    pl.semaphore_wait(barrier, len(greet) + lower)
    pl.when(z > 0)(lambda: signal(ready.at[0], down))
    pl.when(z == Z - 1)(lambda: signal(ready.at[1], up))

    started = []

    def remote(src, dst, send, recv, peer):
        return pltpu.make_async_remote_copy(
            src_ref=src, dst_ref=dst, send_sem=send, recv_sem=recv, device_id=peer, device_id_type=MESH
        )

    def go(copy):
        copy.start()
        started.append(copy)

    def landed(ref, sem):
        pltpu.make_async_copy(ref, ref, sem).wait()

    def held(of_colour):
        low, start_low, start_high = share(z, of_colour)
        always = (1 - y_hi) * 128 * start_low + y_hi * (64 + 128 * (start_high + 2 - low))
        middle = (1 - y_hi) * 128 * (start_low + low - 1) + y_hi * (64 + 128 * start_high)
        rows = [t_ref.at[pl.ds(pl.multiple_of(first + PART * core, PART), PART)] for first in (always, middle)]
        return rows, low + y_hi == 2

    def tile_rows(layer, tile):
        k = (2 * y_hi, 1, 2 - 2 * y_hi)[tile]
        return tbuf.at[layer, core, pl.ds(pl.multiple_of(PART * k, PART), PART)]

    own_rows, own_middle = held(colour)
    out_rows, out_middle = held(partner_colour)
    partner_part = tile_rows(z, 0)
    middle_out = remote(out_rows[1], tile_rows(z, 1), tin_send.at[1], tin_recv.at[1], partner)
    first_up = remote(own_rows[0], tile_rows(z, 0), ring_send.at[0, 0, 0], ring_recv.at[0, 0, 0], up)
    first_down = remote(own_rows[0], tile_rows(z, 0), ring_send.at[1, 0, 0], ring_recv.at[1, 0, 0], down)
    pl.when(z > 0)(first_down.start)
    pl.when(z == Z - 1)(first_up.start)
    go(remote(out_rows[0], partner_part, tin_send.at[2], tin_recv.at[2], partner))
    pl.when(out_middle)(middle_out.start)
    native = pltpu.make_async_copy(own_rows[0], tile_rows(z, 0), tin_recv.at[0])
    native.start()
    pl.when(own_middle)(pltpu.make_async_copy(own_rows[1], tile_rows(z, 1), tin_recv.at[1]).start)

    ahead = (z - colour + Z) % Z
    last = tlast.at[pl.ds(pl.multiple_of(PART * core, PART), PART)]
    last_rows = t_ref.at[pl.ds(pl.multiple_of((1 - core) * 1536, PART), PART)]
    last_out = remote(last_rows, last, last_send.at[2], last_recv.at[0], partner)
    sends_last = (partner_colour == z) & (y_hi == core)
    pl.when(sends_last)(last_out.start)
    pl.when((ahead == 0) & (y_hi == core))(pltpu.make_async_copy(last_rows, last, last_recv.at[0]).start)
    last_up = remote(last, last, last_send.at[0], last_recv.at[0], up)
    last_down = remote(last, last, last_send.at[1], last_recv.at[0], down)
    last_over = remote(last, last, last_send.at[3], last_across.at[0], sibling)

    def pass_last(hop):
        if hop == 0:
            @pl.when(ahead == 0)
            def _():
                landed(last, last_recv.at[0])
                last_up.start()
                last_down.start()
                last_over.start()
            return

        if hop < 4:
            @pl.when(ahead == hop)
            def _():
                landed(last, last_recv.at[0])
                if hop < 3:
                    last_up.start()
                last_over.start()

        @pl.when(ahead == Z - hop)
        def _():
            landed(last, last_recv.at[0])
            if hop < 4:
                last_down.start()
            last_over.start()

    load.wait()

    def pack(pairs, carry):
        for parity in range(2):
            layer = 2 * pairs + parity
            for tile, (of_colour, place) in sorted(tile_places(parity).items()):
                value = raw[pl.ds(TILES * layer + tile, ROWS, stride=LAYERS * TILES), :]
                packed[pl.ds(of_colour * ROWS * TILES + 3 * layer + place, ROWS, stride=TILES), :] = value
            value = raw[pl.ds(TILES * layer + 12, ROWS, stride=LAYERS * TILES), :]
            packed[pl.ds(layer * ROWS * TILES + 24, ROWS, stride=TILES), :] = value
        return carry

    lax.fori_loop(0, LAYERS // 2, pack, 0)

    slots = vbuf.reshape(8, ROWS, TILES, 1, LANES)
    sorted_v = packed.reshape(8, ROWS, TILES, 1, LANES)
    vout = []
    for i in RETURNS:
        step, dx, dy = SENDS[i]
        src = sorted_v.at[(colour + step) % 8]
        vout.append(remote(src, slots.at[i + 1], v_send.at[i], v_recv.at[i], at(dx=dx, dy=dy)))
        vout[-1].start()
    own = pltpu.make_async_copy(sorted_v.at[colour], slots.at[0], v_own.at[0])
    own.start()

    def layer_of(place):
        return (z + PLACES[place] + Z) % Z

    def ring(way, hop, role):
        ref = tile_rows((z - hop + Z) % Z if way == 0 else (z + hop) % Z, role)
        return remote(ref, ref, ring_send.at[way, hop, role], ring_recv.at[way, hop, role], up if way == 0 else down)

    def arrived(way, hop, role):
        landed(tile_rows(layer_of(hop + 1 + 3 * way if hop < 3 else 7), role), ring_recv.at[way, hop, role])

    def across(place):
        ref = tbuf.at[layer_of(place), core]
        return remote(ref, ref, core_send.at[place], core_recv.at[place], sibling)

    @pl.when(z < Z - 1)
    def _():
        pl.semaphore_wait(ready.at[0], 1)
        first_up.start()

    for role in (2, 1):
        landed(tile_rows(z, role), tin_recv.at[role])
        go(ring(0, 0, role))

    @pl.when(z == 0)
    def _():
        pl.semaphore_wait(ready.at[1], 1)
        first_down.start()

    for role in (2, 1):
        go(ring(1, 0, role))
    native.wait()
    go(across(0))
    pass_last(0)
    for hop in range(1, 3):
        for role in (0, 2, 1):
            for way in (1, 0):
                arrived(way, hop - 1, role)
                go(ring(way, hop, role))
        for way in (1, 0):
            go(across(hop + 3 * way))
        pass_last(hop)
    for role in (0, 2, 1):
        arrived(1, 2, role)
        go(ring(1, 3, role))
    go(across(6))

    own.wait()
    for copy in vout:
        copy.wait_recv()

    def split(value):
        high = value.astype(jnp.bfloat16)
        return high, (value - high.astype(jnp.float32)).astype(jnp.bfloat16)

    def product(v, t):
        v_high, v_low = split(v)
        t_high, t_low = split(t)
        dot = functools.partial(jnp.dot, preferred_element_type=jnp.float32)
        return dot(v_high, t_high) + (dot(v_low, t_high) + dot(v_high, t_low))

    def gathered(tile, tiles):
        return jnp.concatenate([vbuf[pl.ds(tile + k, 8 * ROWS, stride=TILES), :] for k in range(tiles)], axis=1)

    def add(place):
        layer = layer_of(place)
        landed(tbuf.at[layer, 1 - core], core_recv.at[place])
        t = [tbuf[layer, c, PART * k : PART * (k + 1), :] for k in range(3) for c in range(2)]
        term = product(gathered(3 * layer, 3), jnp.concatenate(t, axis=0))
        if place == 7:
            return acc[...] + term
        if place == 0:
            acc[...] = term
        else:
            acc[...] += term

    for place in (0, 4, 1, 5, 2):
        add(place)
    for role in (0, 2, 1):
        arrived(0, 2, role)
    go(across(3))
    pass_last(3)
    for role in (0, 2, 1):
        arrived(1, 3, role)
    go(across(7))
    pass_last(4)
    for place in (6, 3):
        add(place)
    landed(tlast.at[pl.ds(pl.multiple_of(PART * (1 - core), PART), PART)], last_across.at[0])
    acc[...] += product(gathered(24, 1), tlast[...])
    final = add(7)

    back = []
    give_rows = give.reshape(7, ROWS, 2, 1, LANES)
    part_rows = parts.reshape(7, ROWS, 2, 1, LANES)
    for i in RETURNS:
        _, dx, dy = SENDS[i]
        for half in range(2):
            value = final[ROWS * (i + 1) : ROWS * (i + 2), LANES * half : LANES * (half + 1)]
            give[pl.ds(2 * ROWS * i + half, ROWS, stride=2), :] = value
        copy = remote(give_rows.at[i], part_rows.at[i], part_send.at[i], part_recv.at[i], at(dx=-dx, dy=-dy))
        copy.start()
        back.append(copy)

    for copy in tables:
        copy.wait()
    lane = lax.broadcasted_iota(jnp.int32, (1, COLS), 1)
    occ_i = jnp.zeros((1, COLS), jnp.float32)
    occ_j = jnp.zeros((1, COLS), jnp.float32)
    for i in range(OCCUPIED):
        occ_i = jnp.where((lane >> 4) == i, occ_ref[i], occ_i)
        occ_j = jnp.where((lane & 15) == i, occ_ref[i], occ_j)
    for s in range(SIDE):
        for t in range(SIDE):
            both = vir_ref[map_ref[0, 0, 0] * SIDE + s] + vir_ref[map_ref[0, 0, 1] * SIDE + t]
            r = s * SIDE + t
            den[r : r + 1, :] = (both - occ_i) - occ_j
    row = lax.broadcasted_iota(jnp.int32, (COLS, COLS), 0)
    col = lax.broadcasted_iota(jnp.int32, (COLS, COLS), 1)
    turn[...] = (((row >> 4) == (col & 15)) & ((row & 15) == (col >> 4))).astype(jnp.bfloat16)

    for copy in vout + started:
        copy.wait_send()
    pl.when(out_middle)(middle_out.wait_send)
    pl.when(sends_last)(last_out.wait_send)
    pl.when(ahead < 3)(last_up.wait_send)
    pl.when((ahead == 0) | (ahead > 4))(last_down.wait_send)
    first_up.wait_send()
    first_down.wait_send()
    last_over.wait_send()
    total = final[0:ROWS, :]
    for i in range(7):
        back[i].wait_recv()
        n = 2 * ROWS * RETURNS[i]
        halves = [parts[pl.ds(n + half, ROWS, stride=2), :] for half in range(2)]
        total = total + jnp.concatenate(halves, axis=1)
    mine[0:ROWS, :] = total
    swap = remote(mine, other, mir_send.at[0], mir_recv.at[0], twin)
    swap.start()
    for copy in back:
        copy.wait_send()
    swap.wait_recv()
    dot = functools.partial(jnp.dot, preferred_element_type=jnp.float32)
    high, rest = split(other[...])
    mid = (other[...] - high.astype(jnp.float32)) - rest.astype(jnp.float32)
    turned = (dot(high, turn[...]) + dot(rest, turn[...])) + dot(mid.astype(jnp.bfloat16), turn[...])
    for s in range(SIDE):
        for t in range(SIDE):
            r, q = s * SIDE + t, t * SIDE + s
            out_ref[r] = (total[r : r + 1] + turned[q : q + 1]) / den[r : r + 1, :]

    swap.wait_send()


def body(integrals, amplitudes, block_map, eps_vir, eps_occ):
    hbm = pl.BlockSpec(memory_space=pltpu.HBM)
    dma = pltpu.SemaphoreType.DMA
    f32 = jnp.float32
    tiles = jnp.transpose(integrals, (0, 2, 1, 3)).reshape(ROWS, 8 * TILES, 1, LANES)
    update = pl.pallas_call(
        kernel,
        out_shape=jax.ShapeDtypeStruct((ROWS, 1, COLS), f32),
        in_specs=[hbm] * 5,
        out_specs=pl.BlockSpec(memory_space=pltpu.VMEM),
        scratch_shapes=[
            pltpu.SMEM((1, 1, 2), jnp.int32),
            pltpu.SMEM((160,), f32),
            pltpu.SMEM((16,), f32),
            dma((3,)),
            pltpu.VMEM((8 * ROWS * TILES, LANES), f32),
            pltpu.VMEM((8 * ROWS * TILES, LANES), f32),
            pltpu.VMEM((8 * ROWS * TILES, LANES), f32),
            pltpu.VMEM((LAYERS, 2, PIECE, COLS), f32),
            pltpu.VMEM((128, COLS), f32),
            pltpu.VMEM((8 * ROWS, COLS), f32),
            pltpu.VMEM((7 * ROWS * 2, LANES), f32),
            pltpu.VMEM((7 * ROWS * 2, LANES), f32),
            pltpu.VMEM((SLOT, COLS), f32),
            pltpu.VMEM((SLOT, COLS), f32),
            pltpu.VMEM((SLOT, COLS), f32),
            pltpu.VMEM((COLS, COLS), jnp.bfloat16),
            pltpu.SemaphoreType.REGULAR((2,)),
            dma((1,)), dma((3,)), dma((3,)),
            dma((2, 4, 3)), dma((2, 4, 3)),
            dma((8,)), dma((8,)),
            dma((4,)), dma((1,)), dma((1,)),
            dma((7,)), dma((7,)), dma((1,)),
            dma((8,)), dma((8,)),
            dma((8,)), dma((8,)),
        ],
        compiler_params=pltpu.CompilerParams(
            collective_id=0, has_side_effects=True, vmem_limit_bytes=56 * 2**20
        ),
        name="ladder",
    )(tiles, amplitudes, block_map, eps_vir, eps_occ)
    return jnp.transpose(update.reshape(1, ROWS, 1, COLS), (0, 2, 1, 3))


def solution(mesh):
    in_specs = (P("blk", "pair", None, None), P("blk", None), P("blk", "pair", None), P(), P())
    out_specs = P("blk", "pair", None, None)
    return jax.shard_map(body, mesh=mesh, in_specs=in_specs, out_specs=out_specs, check_vma=False)
```
